256 devices in a mesh: blk: 16 (over z, y_hi), exp: 16 (over x, y_lo, core).
Axes of the slice: x: 4, y: 4 (y_hi: 2, y_lo: 2; y = y_hi * 2 + y_lo), z: 8, core: 2. Of those that a mesh axis runs over, the one named last changes fastest.
Arguments:
- grad_block: bfloat16 [512, 256, 2048], P('exp', 'blk'), may hold values from -6 to 6
- momentum: float32 [512, 256, 2048], P('exp', 'blk'), may hold values from -6 to 6
- model_root: bfloat16 [2048, 2048], P('blk'), may hold values from -0.125 to 0.125
- expert_root: bfloat16 [512, 512], replicated, may hold values from -0.25 to 0.25
Outputs:
- momentum_new: float32 [512, 256, 2048], P('exp', 'blk')
The draws below stay inside these ranges and needn't reach their ends.
All inputs are finite; a program needn't handle non-finite values.
Results may differ from the reference program's by a relative error of at most 0.0031.
Values may be sent and summed in bfloat16 or wider, within the bound.
No kernel may reach another device: no remote copies, remote signals or barrier semaphores. Data moves between devices by JAX's collectives and lax.ppermute only.
A program may use at most 64 MiB of HBM per device.

```python
import jax
import jax.numpy as jnp

D = 2048
HW = 256
EXPERTS = 512


def levels(rng, dims, cuts, low, largest):
    level, own = 1.0, jax.random.fold_in(rng, 6)
    for dim, shards_of in cuts:
        steps = jnp.exp(jax.random.uniform(jax.random.fold_in(own, dim), (shards_of,), jnp.float32, low / len(cuts), largest / len(cuts)))
        level = level * jnp.repeat(steps, dims[dim] // shards_of).reshape([-1 if axis == dim else 1 for axis in range(len(dims))])
    return level


def bell_draw(stream_key, shape, deviation, most, split=(), held_as=jnp.bfloat16):
    values = deviation * jax.random.normal(stream_key, shape, jnp.float32)
    if split:
        values = values * levels(stream_key, shape, split, -0.22, 0.18)
    return jnp.clip(values, -most, most).astype(held_as)


def setup_inputs(seed: int = 0) -> dict:
    streams_of = jax.random.split(jax.random.key(seed), 5)
    grad_block = bell_draw(streams_of[0], (EXPERTS, HW, D), 1.0, 6.0, ((0, 16), (1, 16)))
    momentum = bell_draw(streams_of[1], (EXPERTS, HW, D), 1.0, 6.0, ((0, 16), (1, 16)), jnp.float32)
    model_root = bell_draw(streams_of[2], (D, D), D ** -0.5, 0.125, ((0, 16),))
    expert_root = bell_draw(streams_of[3], (EXPERTS, EXPERTS), EXPERTS ** -0.5, 0.25)
    return dict(grad_block=grad_block, momentum=momentum, model_root=model_root, expert_root=expert_root)


def reference(grad_block, momentum, model_root, expert_root):
    experts, hidden, width = grad_block.shape
    flat_rows = grad_block.reshape(experts * hidden, width)
    model_mode = jnp.dot(flat_rows, model_root.T, preferred_element_type=jnp.float32).astype(jnp.bfloat16)
    stacked = model_mode.reshape(experts, hidden * width)
    expert_mode = jnp.dot(expert_root, stacked, preferred_element_type=jnp.float32).astype(jnp.bfloat16)
    expert_mode = expert_mode.reshape(experts, hidden, width)
    return 0.9 * momentum + expert_mode.astype(jnp.float32)
```

```python
import jax
import jax.numpy as jnp
from jax import lax
from jax.experimental import pallas as pl
from jax.experimental.pallas import tpu as pltpu
from jax.sharding import Mesh, PartitionSpec as P

NAMES = ("z", "yh", "x", "yl", "core")
SIZES = (8, 2, 4, 2, 2)
EXP = ("x", "yl", "core")
BLK = ("z", "yh")
PARTS = 16
LANES = 128
MIB = 1024 * 1024


def order_matrix(rows, outer, inner, transposed=False):
    first = lax.broadcasted_iota(jnp.int32, (rows, rows), 1 if transposed else 0)
    second = lax.broadcasted_iota(jnp.int32, (rows, rows), 0 if transposed else 1)
    source = (first & (inner - 1)) * outer + lax.div(first, inner)
    return jnp.where(source == second, 1.0, 0.0).astype(jnp.bfloat16)


def slice_kernel(experts, hidden, grad_ref, out_ref, order):
    @pl.when(pl.program_id(0) == 0)
    def _():
        order[...] = order_matrix(experts * hidden, hidden, experts)

    moved = jnp.dot(order[...], grad_ref[...], preferred_element_type=jnp.float32)
    moved = moved.astype(jnp.bfloat16)
    out_ref[0] = moved[:, :LANES]
    out_ref[1] = moved[:, LANES:]


def sliced(grad, experts, hidden):
    rows, width = grad.shape
    return pl.pallas_call(
        lambda *refs: slice_kernel(experts, hidden, *refs),
        out_shape=jax.ShapeDtypeStruct((PARTS, rows, LANES), jnp.bfloat16),
        grid=(PARTS // 2,),
        in_specs=[pl.BlockSpec((rows, 2 * LANES), lambda s: (0, s))],
        out_specs=pl.BlockSpec((2, rows, LANES), lambda s: (s, 0, 0)),
        scratch_shapes=[pltpu.VMEM((rows, rows), jnp.bfloat16)],
        cost_estimate=pl.CostEstimate(
            flops=2 * rows * rows * width, bytes_accessed=4 * rows * width, transcendentals=0
        ),
        name="slice_columns",
    )(grad)


def mix_kernel(root_ref, in_ref, out_ref):
    groups, _, experts, lanes = in_ref.shape
    pair = jnp.concatenate(
        [in_ref[:, 0].reshape(groups * experts, lanes), in_ref[:, 1].reshape(groups * experts, lanes)], axis=1
    )
    mixed = jnp.dot(root_ref[...], pair, preferred_element_type=jnp.float32).astype(jnp.bfloat16)
    out_ref[:, 0] = mixed[:, :lanes].reshape(groups, experts, lanes)
    out_ref[:, 1] = mixed[:, lanes:].reshape(groups, experts, lanes)


def mixed_experts(expert_root, held):
    groups, hidden, experts, lanes = held.shape
    block = pl.BlockSpec((groups, 2, experts, lanes), lambda s: (0, s, 0, 0))
    total = groups * experts
    return pl.pallas_call(
        mix_kernel,
        out_shape=jax.ShapeDtypeStruct(held.shape, jnp.bfloat16),
        grid=(hidden // 2,),
        in_specs=[pl.BlockSpec((total, total), lambda s: (0, 0)), block],
        out_specs=block,
        cost_estimate=pl.CostEstimate(
            flops=2 * total * total * hidden * lanes, bytes_accessed=4 * total * hidden * lanes, transcendentals=0
        ),
        name="mix_experts",
    )(expert_root, held)


def finish_kernel(experts, hidden, yh_ref, held_ref, root_ref, momentum_ref, out_ref, rows_ref):
    half = root_ref.shape[-1]
    per_half = half // LANES
    rows = experts * hidden

    @pl.when(pl.program_id(0) == 0)
    def _():
        order = order_matrix(rows, hidden, experts, transposed=True)
        for part in range(0, PARTS, 2):
            pair = jnp.concatenate([held_ref[part], held_ref[part + 1]], axis=1)
            moved = jnp.dot(order, pair, preferred_element_type=jnp.float32).astype(jnp.bfloat16)
            at = (part % per_half) * LANES
            rows_ref[part // per_half, :, at : at + 2 * LANES] = moved

    yh = yh_ref[0]
    total = 0.9 * momentum_ref[...]
    for which in range(2):
        root = jnp.concatenate([root_ref[which, 0, yh], root_ref[which, 0, 1 - yh]], axis=0)
        total += lax.dot_general(
            rows_ref[which], root, (((1,), (1,)), ((), ())), preferred_element_type=jnp.float32
        )
    out_ref[...] = total


def finished(yh, held, root, momentum, experts, hidden):
    parts, rows, lanes = held.shape
    halves, steps, pair, block, half = root.shape
    columns = pair * block
    width = steps * columns
    out_spec = pl.BlockSpec((rows, columns), lambda s, yh: (0, s))
    return pl.pallas_call(
        lambda *refs: finish_kernel(experts, hidden, *refs),
        out_shape=jax.ShapeDtypeStruct(momentum.shape, jnp.float32),
        grid_spec=pltpu.PrefetchScalarGridSpec(
            num_scalar_prefetch=1,
            grid=(steps,),
            in_specs=[
                pl.BlockSpec((parts, rows, lanes), lambda s, yh: (0, 0, 0)),
                pl.BlockSpec((halves, 1, pair, block, half), lambda s, yh: (0, s, 0, 0, 0)),
                out_spec,
            ],
            out_specs=out_spec,
            scratch_shapes=[pltpu.VMEM((halves, rows, half), jnp.bfloat16)],
        ),
        compiler_params=pltpu.CompilerParams(vmem_limit_bytes=40 * MIB),
        cost_estimate=pl.CostEstimate(
            flops=2 * rows * width * (width + rows), bytes_accessed=2 * width * width + 10 * rows * width, transcendentals=0
        ),
        name="model_rows",
    )(yh, held, root, momentum)


def swap(value, axis):
    return lax.ppermute(value, axis, [(0, 1), (1, 0)])


def per_device(grad_block, momentum, model_root, expert_root):
    experts, hidden, width = grad_block.shape
    rows = experts * hidden
    half = width // 2
    yh, core = lax.axis_index("yh"), lax.axis_index("core")

    mine = lax.dynamic_slice_in_dim(model_root, core * half, half, axis=1)
    both = jnp.stack([mine, swap(mine, "yh")])
    root = lax.all_gather(both, ("core", "z"), axis=0).reshape(2, SIZES[0], 2, -1, half)

    sent = sliced(grad_block.reshape(rows, width), experts, hidden)
    held = lax.all_to_all(sent, EXP, split_axis=0, concat_axis=0, tiled=True)
    blended = mixed_experts(expert_root, held.reshape(PARTS, hidden, experts, LANES))
    back = lax.all_to_all(
        blended.reshape(PARTS, rows, LANES), EXP, split_axis=0, concat_axis=0, tiled=True
    )
    place = yh.astype(jnp.int32)[None]
    out = finished(place, back, root, momentum.reshape(rows, width), experts, hidden)
    return out.reshape(experts, hidden, width)


def solution(mesh):
    fine = Mesh(mesh.devices.reshape(SIZES), NAMES)
    placed = (P(EXP, BLK, None), P(EXP, BLK, None), P(BLK, None), P())
    return jax.shard_map(
        per_device, mesh=fine, in_specs=placed, out_specs=P(EXP, BLK, None), check_vma=False
    )
```

```python
import jax
import jax.numpy as jnp
from jax import lax
from jax.experimental import pallas as pl
from jax.experimental.pallas import tpu as pltpu
from jax.sharding import Mesh, PartitionSpec as P

NAMES = ("z", "yh", "x", "yl", "core")
SIZES = (8, 2, 4, 2, 2)
EXP = ("x", "yl", "core")
BLK = ("z", "yh")
PARTS = 16
LANES = 128
MIB = 1024 * 1024
OFFSETS = (0, 1, -1, 2, -2, 3, -3, 4)
VMEM = pl.BlockSpec(memory_space=pltpu.VMEM)
ANY = pl.BlockSpec(memory_space=pl.ANY)


def order_matrix(rows, outer, inner):
    row = lax.broadcasted_iota(jnp.int32, (rows, 1), 0)
    source = (row & (outer - 1)) * inner + lax.shift_right_logical(row, outer.bit_length() - 1)
    column = lax.broadcasted_iota(jnp.int32, (rows, rows), 1)
    return jnp.where(source == column, 1.0, 0.0).astype(jnp.bfloat16)


def slice_kernel(experts, hidden, grad_ref, out_ref, grad, parts, in_sems, out_sems):
    pairs = PARTS // 2

    def arrival(pair):
        columns = pl.ds(pair * 2 * LANES, 2 * LANES)
        return pltpu.make_async_copy(grad_ref.at[:, columns], grad.at[pair], in_sems.at[pair])

    def departure(pair):
        both = pl.ds(2 * pair, 2)
        return pltpu.make_async_copy(parts.at[both], out_ref.at[both], out_sems.at[pair])

    for pair in range(pairs):
        arrival(pair).start()
    order = order_matrix(experts * hidden, experts, hidden)
    for pair in range(pairs):
        arrival(pair).wait()
        moved = jnp.dot(order, grad[pair], preferred_element_type=jnp.float32).astype(jnp.bfloat16)
        parts[2 * pair] = moved[:, :LANES]
        parts[2 * pair + 1] = moved[:, LANES:]
        departure(pair).start()
    for pair in range(pairs):
        departure(pair).wait()


def sliced(grad, experts, hidden):
    rows, width = grad.shape
    pairs = PARTS // 2
    return pl.pallas_call(
        lambda *refs: slice_kernel(experts, hidden, *refs),
        out_shape=jax.ShapeDtypeStruct((PARTS, rows, LANES), jnp.bfloat16),
        in_specs=[ANY],
        out_specs=ANY,
        scratch_shapes=[
            pltpu.VMEM((pairs, rows, 2 * LANES), jnp.bfloat16),
            pltpu.VMEM((PARTS, rows, LANES), jnp.bfloat16),
            pltpu.SemaphoreType.DMA((pairs,)),
            pltpu.SemaphoreType.DMA((pairs,)),
        ],
        compiler_params=pltpu.CompilerParams(vmem_limit_bytes=58 * MIB),
        cost_estimate=pl.CostEstimate(
            flops=2 * rows * rows * width, bytes_accessed=4 * rows * width, transcendentals=0
        ),
        name="slice_columns",
    )(grad)


def mix_kernel(root_ref, in_ref, out_ref, root, mixed, in_sem, out_sems):
    groups, hidden, experts, lanes = in_ref.shape

    def departure(h):
        there = (slice(None), pl.ds(h, 2))
        return pltpu.make_async_copy(mixed.at[there], out_ref.at[there], out_sems.at[h // 2])

    arrival = pltpu.make_async_copy(root_ref, root, in_sem)
    arrival.start()
    arrival.wait()
    for h in range(0, hidden, 2):
        pair = jnp.concatenate(
            [in_ref[:, at].reshape(groups * experts, lanes) for at in (h, h + 1)], axis=1
        )
        sums = jnp.dot(root[...], pair, preferred_element_type=jnp.float32).astype(jnp.bfloat16)
        mixed[:, h] = sums[:, :lanes].reshape(groups, experts, lanes)
        mixed[:, h + 1] = sums[:, lanes:].reshape(groups, experts, lanes)
        departure(h).start()
    for h in range(0, hidden, 2):
        departure(h).wait()


def mixed_experts(expert_root, held):
    groups, hidden, experts, lanes = held.shape
    total = groups * experts
    return pl.pallas_call(
        mix_kernel,
        out_shape=jax.ShapeDtypeStruct(held.shape, jnp.bfloat16),
        in_specs=[ANY, VMEM],
        out_specs=ANY,
        scratch_shapes=[
            pltpu.VMEM((total, total), jnp.bfloat16),
            pltpu.VMEM(held.shape, jnp.bfloat16),
            pltpu.SemaphoreType.DMA,
            pltpu.SemaphoreType.DMA((hidden // 2,)),
        ],
        compiler_params=pltpu.CompilerParams(vmem_limit_bytes=24 * MIB),
        cost_estimate=pl.CostEstimate(
            flops=2 * total * total * hidden * lanes, bytes_accessed=4 * total * hidden * lanes, transcendentals=0
        ),
        name="mix_experts",
    )(expert_root, held)


def finish_kernel(experts, hidden, pieces, place_ref, held_ref, *refs):
    sources = refs[:pieces], refs[pieces : 2 * pieces]
    momentum_ref, out_ref, held_parts, roots, momentum, out, sums = refs[2 * pieces : 2 * pieces + 7]
    held_sem, root_sems, momentum_sems, out_sems = refs[2 * pieces + 7 :]
    steps, rows, columns = out.shape
    per_half = PARTS // 2
    yh, core = place_ref[0], place_ref[1]

    def block(ref, step):
        return ref.at[:, pl.ds(pl.multiple_of(place_ref[2 + step] * columns, columns), columns)]

    def root_arrivals(side, step):
        pieces_of, sem = sources[side], root_sems.at[side]
        if step < steps - 1:
            return [pltpu.make_async_copy(pieces_of[step], roots.at[side, step], sem.at[step])]
        return [
            pltpu.make_async_copy(pieces_of[step + k], roots.at[side, step, k], sem.at[step + k]) for k in range(2)
        ]

    def momentum_arrival(step):
        return pltpu.make_async_copy(block(momentum_ref, step), momentum.at[step], momentum_sems.at[step])

    def departure(step):
        return pltpu.make_async_copy(out.at[step], block(out_ref, step), out_sems.at[step])

    held_arrival = pltpu.make_async_copy(held_ref, held_parts, held_sem)
    held_arrival.start()
    for step in range(steps):
        for copy in (*root_arrivals(0, step), *root_arrivals(1, step), momentum_arrival(step)):
            copy.start()
    held_arrival.wait()
    for step in range(steps):
        total = None
        for side, which in ((0, core), (1, 1 - core)):
            for copy in root_arrivals(side, step):
                copy.wait()
            held = jnp.concatenate([held_parts[which * per_half + part] for part in range(per_half)], axis=1)
            root = roots[side, step].reshape(columns, per_half * LANES)
            term = lax.dot_general(held, root, (((1,), (1,)), ((), ())), preferred_element_type=jnp.float32)
            total = term if total is None else total + term
        sums[yh] = total[:, :LANES]
        sums[1 - yh] = total[:, LANES:]
        momentum_arrival(step).wait()
        for tile in range(columns // LANES):
            lanes = slice(tile * LANES, (tile + 1) * LANES)
            for expert in range(experts):
                there = slice(expert * hidden, (expert + 1) * hidden)
                change = sums[tile, pl.ds(expert, hidden, stride=experts), :]
                out[step, there, lanes] = 0.9 * momentum[step, there, lanes] + change
        departure(step).start()
    for step in range(steps):
        departure(step).wait()


def finished(place, held, own, other, momentum, experts, hidden):
    parts, rows, lanes = held.shape
    width = parts * lanes
    columns = 2 * LANES
    pieces, steps = len(own), len(OFFSETS)
    return pl.pallas_call(
        lambda *refs: finish_kernel(experts, hidden, pieces, *refs),
        out_shape=jax.ShapeDtypeStruct(momentum.shape, jnp.float32),
        in_specs=[pl.BlockSpec(memory_space=pltpu.SMEM), ANY, *[ANY] * (2 * pieces), ANY],
        out_specs=ANY,
        scratch_shapes=[
            pltpu.VMEM(held.shape, jnp.bfloat16),
            pltpu.VMEM((2, steps, *own[0].shape), jnp.bfloat16),
            pltpu.VMEM((steps, rows, columns), jnp.float32),
            pltpu.VMEM((steps, rows, columns), jnp.float32),
            pltpu.VMEM((2, rows, LANES), jnp.float32),
            pltpu.SemaphoreType.DMA,
            pltpu.SemaphoreType.DMA((2, pieces)),
            pltpu.SemaphoreType.DMA((steps,)),
            pltpu.SemaphoreType.DMA((steps,)),
        ],
        compiler_params=pltpu.CompilerParams(vmem_limit_bytes=52 * MIB),
        cost_estimate=pl.CostEstimate(
            flops=2 * rows * width * width, bytes_accessed=2 * width * width + 10 * rows * width, transcendentals=0
        ),
        name="model_rows",
    )(place, held, *own, *other, momentum)


def swap(value, axis):
    return lax.ppermute(value, axis, [(0, 1), (1, 0)])


def along_z(value, step):
    n = SIZES[0]
    return lax.ppermute(value, "z", [(i, (i + step) % n) for i in range(n)])


def exchange(value):
    return lax.all_to_all(value, EXP, split_axis=0, concat_axis=0, tiled=True)


def per_device(grad_block, momentum, model_root, expert_root):
    experts, hidden, width = grad_block.shape
    rows = experts * hidden
    half = width // 2
    z, yh, core = (lax.axis_index(axis) for axis in ("z", "yh", "core"))

    mine = lax.dynamic_slice_in_dim(model_root, core * half, half, axis=1)
    theirs = swap(mine, "yh")
    sent = sliced(grad_block.reshape(rows, width), experts, hidden)
    mine, theirs, sent = lax.optimization_barrier((mine, theirs, sent))

    held = exchange(sent)
    here = jnp.stack([mine, theirs])
    up1, down1 = along_z(here, 1), along_z(here, -1)
    up2, down2 = along_z(up1, 1), along_z(down1, -1)
    near = (here, down1, up1)
    others = tuple(swap(piece, "core") for piece in near)
    held, up2, down2, others = lax.optimization_barrier((held, up2, down2, others))

    blended = mixed_experts(expert_root, held.reshape(PARTS, hidden, experts, LANES))
    blended, up2, down2 = lax.optimization_barrier((blended, up2, down2))

    back = exchange(blended.reshape(PARTS, rows, LANES))
    up3, down3 = along_z(up2, 1), along_z(down2, -1)
    late = (down2, up2, down3, up3, along_z(up2[0], 2), along_z(down2[1], -2))
    own = near + late
    other = others + tuple(swap(piece, "core") for piece in late)

    order = [lax.rem(z + SIZES[0] + offset, SIZES[0]) for offset in OFFSETS]
    place = jnp.stack([yh, core, *order]).astype(jnp.int32)
    out = finished(place, back, own, other, momentum.reshape(rows, width), experts, hidden)
    return out.reshape(experts, hidden, width)


def solution(mesh):
    fine = Mesh(mesh.devices.reshape(SIZES), NAMES)
    placed = (P(EXP, BLK, None), P(EXP, BLK, None), P(BLK, None), P())
    return jax.shard_map(
        per_device, mesh=fine, in_specs=placed, out_specs=P(EXP, BLK, None), check_vma=False
    )
```

```python
import jax
import jax.numpy as jnp
from jax import lax
from jax.experimental import pallas as pl
from jax.experimental.pallas import tpu as pltpu
from jax.sharding import Mesh, PartitionSpec as P

NAMES = ("z", "yh", "x", "yl", "core")
SIZES = (8, 2, 4, 2, 2)
EXP = ("x", "yl", "core")
BLK = ("z", "yh")
PARTS = 16
GROUP = 4
LANES = 128
MIB = 1024 * 1024
OFFSETS = (0, 1, -1, 2, -2, 3, -3, 4)
VMEM = pl.BlockSpec(memory_space=pltpu.VMEM)
ANY = pl.BlockSpec(memory_space=pl.ANY)


def order_matrix(rows, outer, inner):
    row = lax.broadcasted_iota(jnp.int32, (rows, 1), 0)
    source = (row & (outer - 1)) * inner + lax.shift_right_logical(row, outer.bit_length() - 1)
    column = lax.broadcasted_iota(jnp.int32, (rows, rows), 1)
    return jnp.where(source == column, 1.0, 0.0).astype(jnp.bfloat16)


def slice_kernel(grad_ref, out_ref, parts, in_sems, out_sems):
    def arrival(part):
        return pltpu.make_async_copy(grad_ref.at[:, pl.ds(part * LANES, LANES)], parts.at[part], in_sems.at[part])

    def departure(part):
        return pltpu.make_async_copy(parts.at[part], out_ref.at[part], out_sems.at[part])

    for part in range(PARTS):
        arrival(part).start()
    for part in range(PARTS):
        arrival(part).wait()
        departure(part).start()
    for part in range(PARTS):
        departure(part).wait()


def sliced(grad):
    rows, width = grad.shape
    shape = (PARTS, rows, LANES)
    return pl.pallas_call(
        slice_kernel,
        out_shape=jax.ShapeDtypeStruct(shape, jnp.bfloat16),
        in_specs=[ANY],
        out_specs=ANY,
        scratch_shapes=[
            pltpu.VMEM(shape, jnp.bfloat16),
            pltpu.SemaphoreType.DMA((PARTS,)),
            pltpu.SemaphoreType.DMA((PARTS,)),
        ],
        compiler_params=pltpu.CompilerParams(vmem_limit_bytes=58 * MIB),
        cost_estimate=pl.CostEstimate(flops=0, bytes_accessed=4 * rows * width, transcendentals=0),
        name="slice_columns",
    )(grad)


def mix_kernel(experts, hidden, root_ref, in_ref, out_ref, root, turned, mixed, in_sem, out_sems):
    groups, rows, lanes = in_ref.shape

    def departure(h):
        there = (slice(None), pl.ds(h, GROUP))
        return pltpu.make_async_copy(mixed.at[there], out_ref.at[there], out_sems.at[h // GROUP])

    arrival = pltpu.make_async_copy(root_ref, root, in_sem)
    arrival.start()
    order = order_matrix(rows, experts, hidden)
    for group in range(0, groups, GROUP):
        some = jnp.concatenate([in_ref[group + k] for k in range(GROUP)], axis=1)
        moved = jnp.dot(order, some, preferred_element_type=jnp.float32).astype(jnp.bfloat16)
        for k in range(GROUP):
            at = slice((group + k) * experts, (group + k + 1) * experts)
            turned[:, at] = moved[:, k * lanes : (k + 1) * lanes].reshape(hidden, experts, lanes)
    arrival.wait()
    for h in range(0, hidden, GROUP):
        some = jnp.concatenate([turned[h + k] for k in range(GROUP)], axis=1)
        sums = jnp.dot(root[...], some, preferred_element_type=jnp.float32).astype(jnp.bfloat16)
        for k in range(GROUP):
            mixed[:, h + k] = sums[:, k * lanes : (k + 1) * lanes].reshape(groups, experts, lanes)
        departure(h).start()
    for h in range(0, hidden, GROUP):
        departure(h).wait()


def mixed_experts(expert_root, held, experts, hidden):
    groups, rows, lanes = held.shape
    total = groups * experts
    shape = (groups, hidden, experts, lanes)
    return pl.pallas_call(
        lambda *refs: mix_kernel(experts, hidden, *refs),
        out_shape=jax.ShapeDtypeStruct(shape, jnp.bfloat16),
        in_specs=[ANY, VMEM],
        out_specs=ANY,
        scratch_shapes=[
            pltpu.VMEM((total, total), jnp.bfloat16),
            pltpu.VMEM((hidden, total, lanes), jnp.bfloat16),
            pltpu.VMEM(shape, jnp.bfloat16),
            pltpu.SemaphoreType.DMA,
            pltpu.SemaphoreType.DMA((hidden // GROUP,)),
        ],
        compiler_params=pltpu.CompilerParams(vmem_limit_bytes=24 * MIB),
        cost_estimate=pl.CostEstimate(flops=0, bytes_accessed=0, transcendentals=0),
        name="mix_experts",
    )(expert_root, held)


def finish_kernel(experts, hidden, pieces, place_ref, held_ref, *refs):
    sources = refs[:pieces], refs[pieces : 2 * pieces]
    momentum_ref, out_ref, held, rows_of, roots, momentum, out = refs[2 * pieces : 2 * pieces + 7]
    held_sem, root_sems, momentum_sems, out_sems = refs[2 * pieces + 7 :]
    steps, rows, columns = out.shape
    per_half = PARTS // 2
    yh, core = place_ref[0], place_ref[1]

    def block(ref, step):
        return ref.at[:, pl.ds(pl.multiple_of(place_ref[2 + step] * columns, columns), columns)]

    def root_arrivals(side, step):
        pieces_of, sem = sources[side], root_sems.at[side]
        if step < steps - 1:
            return [pltpu.make_async_copy(pieces_of[step], roots.at[side, step], sem.at[step])]
        return [
            pltpu.make_async_copy(pieces_of[step + k], roots.at[side, step, k], sem.at[step + k]) for k in range(2)
        ]

    def momentum_arrival(step):
        return pltpu.make_async_copy(block(momentum_ref, step), momentum.at[step], momentum_sems.at[step])

    def departure(step):
        return pltpu.make_async_copy(out.at[step], block(out_ref, step), out_sems.at[step])

    held_arrival = pltpu.make_async_copy(held_ref, held, held_sem)
    held_arrival.start()
    for step in range(steps):
        for copy in (*root_arrivals(0, step), *root_arrivals(1, step), momentum_arrival(step)):
            copy.start()
    order = order_matrix(rows, hidden, experts)
    held_arrival.wait()
    for part in range(0, PARTS, GROUP):
        some = jnp.concatenate([held[part + k] for k in range(GROUP)], axis=1)
        moved = jnp.dot(order, some, preferred_element_type=jnp.float32).astype(jnp.bfloat16)
        at = (part % per_half) * LANES
        rows_of[part // per_half, :, at : at + GROUP * LANES] = moved
    for first in range(0, steps, 2):
        both = (first, first + 1)
        total = None
        for side, which in ((0, core), (1, 1 - core)):
            for step in both:
                for copy in root_arrivals(side, step):
                    copy.wait()
            root = jnp.concatenate([roots[side, step, k] for step in both for k in range(2)], axis=1)
            term = jnp.dot(rows_of[which], root, preferred_element_type=jnp.float32)
            total = term if total is None else total + term
        for step in both:
            momentum_arrival(step).wait()
            for k, block_at in ((0, yh), (1, 1 - yh)):
                lanes = pl.ds(pl.multiple_of(block_at * LANES, LANES), LANES)
                at = ((step - first) * 2 + k) * LANES
                out[step, :, lanes] = 0.9 * momentum[step, :, lanes] + total[:, at : at + LANES]
            departure(step).start()
    for step in range(steps):
        departure(step).wait()


def finished(place, held, own, other, momentum, experts, hidden):
    parts, rows, lanes = held.shape
    width = parts * lanes
    columns = 2 * LANES
    pieces, steps = len(own), len(OFFSETS)
    return pl.pallas_call(
        lambda *refs: finish_kernel(experts, hidden, pieces, *refs),
        out_shape=jax.ShapeDtypeStruct(momentum.shape, jnp.float32),
        in_specs=[pl.BlockSpec(memory_space=pltpu.SMEM), ANY, *[ANY] * (2 * pieces), ANY],
        out_specs=ANY,
        scratch_shapes=[
            pltpu.VMEM(held.shape, jnp.bfloat16),
            pltpu.VMEM((2, rows, width // 2), jnp.bfloat16),
            pltpu.VMEM((2, steps, *own[0].shape), jnp.bfloat16),
            pltpu.VMEM((steps, rows, columns), jnp.float32),
            pltpu.VMEM((steps, rows, columns), jnp.float32),
            pltpu.SemaphoreType.DMA,
            pltpu.SemaphoreType.DMA((2, pieces)),
            pltpu.SemaphoreType.DMA((steps,)),
            pltpu.SemaphoreType.DMA((steps,)),
        ],
        compiler_params=pltpu.CompilerParams(vmem_limit_bytes=52 * MIB),
        cost_estimate=pl.CostEstimate(
            flops=2 * rows * width * width, bytes_accessed=2 * width * width + 10 * rows * width, transcendentals=0
        ),
        name="model_rows",
    )(place, held, *own, *other, momentum)


def swap(value, axis):
    return lax.ppermute(value, axis, [(0, 1), (1, 0)])


def along_z(value, step):
    n = SIZES[0]
    return lax.ppermute(value, "z", [(i, (i + step) % n) for i in range(n)])


def exchange(value):
    return lax.all_to_all(value, EXP, split_axis=0, concat_axis=0, tiled=True)


def per_device(grad_block, momentum, model_root, expert_root):
    experts, hidden, width = grad_block.shape
    rows = experts * hidden
    half = width // 2
    z, yh, core = (lax.axis_index(axis) for axis in ("z", "yh", "core"))

    mine = lax.dynamic_slice_in_dim(model_root, core * half, half, axis=1).T
    theirs = swap(mine, "yh")
    here = jnp.stack([mine, theirs])
    sent = sliced(grad_block.reshape(rows, width))
    here, sent = lax.optimization_barrier((here, sent))

    held = exchange(sent)
    up1, down1 = along_z(here, 1), along_z(here, -1)
    first = (swap(here, "core"),)
    held, first, _, _ = lax.optimization_barrier((held, first, up1, down1))

    up2, down2 = along_z(up1, 1), along_z(down1, -1)
    blended = mixed_experts(expert_root, held, experts, hidden)
    second = (swap(down1, "core"), swap(up1, "core"))
    blended, up2, down2, second = lax.optimization_barrier((blended, up2, down2, second))

    back = exchange(blended.reshape(PARTS, rows, LANES))
    up3, down3 = along_z(up2, 1), along_z(down2, -1)
    own = (here, down1, up1, down2, up2, down3, up3, along_z(up3[0], 1), along_z(down3[1], -1))
    other = first + second + tuple(swap(piece, "core") for piece in own[3:])

    order = [lax.rem(z + SIZES[0] + offset, SIZES[0]) for offset in OFFSETS]
    place = jnp.stack([yh, core, *order]).astype(jnp.int32)
    out = finished(place, back, own, other, momentum.reshape(rows, width), experts, hidden)
    return out.reshape(experts, hidden, width)


def solution(mesh):
    fine = Mesh(mesh.devices.reshape(SIZES), NAMES)
    placed = (P(EXP, BLK, None), P(EXP, BLK, None), P(BLK, None), P())
    return jax.shard_map(
        per_device, mesh=fine, in_specs=placed, out_specs=P(EXP, BLK, None), check_vma=False
    )
```

```python
import jax
import jax.numpy as jnp
from jax import lax
from jax.experimental import pallas as pl
from jax.experimental.pallas import tpu as pltpu
from jax.sharding import Mesh, PartitionSpec as P

NAMES = ("z", "yh", "x", "yl", "core")
SIZES = (8, 2, 4, 2, 2)
EXP = ("x", "yl", "core")
BLK = ("z", "yh")
PARTS = 16
GROUP = 4
LANES = 128
MIB = 1024 * 1024
OFFSETS = (0, 1, -1, 2, -2, 3, -3, 4)
VMEM = pl.BlockSpec(memory_space=pltpu.VMEM)
ANY = pl.BlockSpec(memory_space=pl.ANY)


def order_matrix(rows, outer, inner):
    row = lax.broadcasted_iota(jnp.int32, (rows, 1), 0)
    source = (row & (outer - 1)) * inner + lax.shift_right_logical(row, outer.bit_length() - 1)
    column = lax.broadcasted_iota(jnp.int32, (rows, rows), 1)
    return jnp.where(source == column, 1.0, 0.0).astype(jnp.bfloat16)


def slice_kernel(experts, hidden, grad_ref, out_ref, grad, parts, in_sems, out_sems):
    groups, rows, columns = grad.shape

    def arrival(group):
        lanes = pl.ds(group * columns, columns)
        return pltpu.make_async_copy(grad_ref.at[:, lanes], grad.at[group], in_sems.at[group])

    def departure(group):
        there = pl.ds(group * GROUP, GROUP)
        return pltpu.make_async_copy(parts.at[there], out_ref.at[there], out_sems.at[group])

    for group in range(groups):
        arrival(group).start()
    order = order_matrix(rows, experts, hidden)
    for group in range(groups):
        arrival(group).wait()
        moved = jnp.dot(order, grad[group], preferred_element_type=jnp.float32).astype(jnp.bfloat16)
        for k in range(GROUP):
            parts[group * GROUP + k] = moved[:, k * LANES : (k + 1) * LANES]
        departure(group).start()
    for group in range(groups):
        departure(group).wait()


def sliced(grad, experts, hidden):
    rows, width = grad.shape
    groups = PARTS // GROUP
    shape = (PARTS, rows, LANES)
    return pl.pallas_call(
        lambda *refs: slice_kernel(experts, hidden, *refs),
        out_shape=jax.ShapeDtypeStruct(shape, jnp.bfloat16),
        in_specs=[ANY],
        out_specs=ANY,
        scratch_shapes=[
            pltpu.VMEM((groups, rows, GROUP * LANES), jnp.bfloat16),
            pltpu.VMEM(shape, jnp.bfloat16),
            pltpu.SemaphoreType.DMA((groups,)),
            pltpu.SemaphoreType.DMA((groups,)),
        ],
        compiler_params=pltpu.CompilerParams(vmem_limit_bytes=58 * MIB),
        cost_estimate=pl.CostEstimate(
            flops=2 * rows * rows * width, bytes_accessed=4 * rows * width, transcendentals=0
        ),
        name="slice_columns",
    )(grad)


def mix_kernel(root_ref, in_ref, out_ref, root, mixed, in_sem, out_sems):
    groups, hidden, experts, lanes = in_ref.shape

    def departure(h):
        there = (slice(None), pl.ds(h, GROUP))
        return pltpu.make_async_copy(mixed.at[there], out_ref.at[there], out_sems.at[h // GROUP])

    arrival = pltpu.make_async_copy(root_ref, root, in_sem)
    arrival.start()
    arrival.wait()
    for h in range(0, hidden, GROUP):
        some = jnp.concatenate([in_ref[:, h + k].reshape(groups * experts, lanes) for k in range(GROUP)], axis=1)
        sums = jnp.dot(root[...], some, preferred_element_type=jnp.float32).astype(jnp.bfloat16)
        for k in range(GROUP):
            mixed[:, h + k] = sums[:, k * lanes : (k + 1) * lanes].reshape(groups, experts, lanes)
        departure(h).start()
    for h in range(0, hidden, GROUP):
        departure(h).wait()


def mixed_experts(expert_root, held):
    groups, hidden, experts, lanes = held.shape
    total = groups * experts
    return pl.pallas_call(
        mix_kernel,
        out_shape=jax.ShapeDtypeStruct(held.shape, jnp.bfloat16),
        in_specs=[ANY, VMEM],
        out_specs=ANY,
        scratch_shapes=[
            pltpu.VMEM((total, total), jnp.bfloat16),
            pltpu.VMEM(held.shape, jnp.bfloat16),
            pltpu.SemaphoreType.DMA,
            pltpu.SemaphoreType.DMA((hidden // GROUP,)),
        ],
        compiler_params=pltpu.CompilerParams(vmem_limit_bytes=24 * MIB),
        cost_estimate=pl.CostEstimate(flops=0, bytes_accessed=0, transcendentals=0),
        name="mix_experts",
    )(expert_root, held)


def finish_kernel(experts, hidden, pieces, place_ref, held_ref, *refs):
    sources = refs[:pieces], refs[pieces : 2 * pieces]
    momentum_ref, out_ref, held, rows_of, roots, momentum, out = refs[2 * pieces : 2 * pieces + 7]
    held_sem, root_sems, momentum_sems, out_sems = refs[2 * pieces + 7 :]
    steps, rows, columns = out.shape
    per_half = PARTS // 2
    yh, core = place_ref[0], place_ref[1]

    def block(ref, step):
        return ref.at[:, pl.ds(pl.multiple_of(place_ref[2 + step] * columns, columns), columns)]

    def root_arrivals(side, step):
        pieces_of, sem = sources[side], root_sems.at[side]
        return [
            pltpu.make_async_copy(pieces_of[2 * step + k], roots.at[side, step, k], sem.at[2 * step + k])
            for k in range(2)
        ]

    def momentum_arrival(step):
        return pltpu.make_async_copy(block(momentum_ref, step), momentum.at[step], momentum_sems.at[step])

    def departure(step):
        return pltpu.make_async_copy(out.at[step], block(out_ref, step), out_sems.at[step])

    held_arrival = pltpu.make_async_copy(held_ref, held, held_sem)
    held_arrival.start()
    for step in range(steps):
        for copy in (*root_arrivals(0, step), *root_arrivals(1, step), momentum_arrival(step)):
            copy.start()
    order = order_matrix(rows, hidden, experts)
    held_arrival.wait()
    for part in range(0, PARTS, GROUP):
        some = jnp.concatenate([held[part + k] for k in range(GROUP)], axis=1)
        moved = jnp.dot(order, some, preferred_element_type=jnp.float32).astype(jnp.bfloat16)
        at = (part % per_half) * LANES
        rows_of[part // per_half, :, at : at + GROUP * LANES] = moved
    for first in range(0, steps, 2):
        both = (first, first + 1)
        total = None
        for side, which in ((0, core), (1, 1 - core)):
            for step in both:
                for copy in root_arrivals(side, step):
                    copy.wait()
            root = jnp.concatenate([roots[side, step, k] for step in both for k in range(2)], axis=1)
            term = jnp.dot(rows_of[which], root, preferred_element_type=jnp.float32)
            total = term if total is None else total + term
        for step in both:
            momentum_arrival(step).wait()
            for k, block_at in ((0, yh), (1, 1 - yh)):
                lanes = pl.ds(pl.multiple_of(block_at * LANES, LANES), LANES)
                at = ((step - first) * 2 + k) * LANES
                out[step, :, lanes] = 0.9 * momentum[step, :, lanes] + total[:, at : at + LANES]
            departure(step).start()
    for step in range(steps):
        departure(step).wait()


def finished(place, held, own, other, momentum, experts, hidden):
    parts, rows, lanes = held.shape
    width = parts * lanes
    columns = 2 * LANES
    pieces, steps = len(own), len(OFFSETS)
    return pl.pallas_call(
        lambda *refs: finish_kernel(experts, hidden, pieces, *refs),
        out_shape=jax.ShapeDtypeStruct(momentum.shape, jnp.float32),
        in_specs=[pl.BlockSpec(memory_space=pltpu.SMEM), ANY, *[ANY] * (2 * pieces), ANY],
        out_specs=ANY,
        scratch_shapes=[
            pltpu.VMEM(held.shape, jnp.bfloat16),
            pltpu.VMEM((2, rows, width // 2), jnp.bfloat16),
            pltpu.VMEM((2, steps, 2, *own[0].shape), jnp.bfloat16),
            pltpu.VMEM((steps, rows, columns), jnp.float32),
            pltpu.VMEM((steps, rows, columns), jnp.float32),
            pltpu.SemaphoreType.DMA,
            pltpu.SemaphoreType.DMA((2, pieces)),
            pltpu.SemaphoreType.DMA((steps,)),
            pltpu.SemaphoreType.DMA((steps,)),
        ],
        compiler_params=pltpu.CompilerParams(vmem_limit_bytes=52 * MIB),
        cost_estimate=pl.CostEstimate(
            flops=2 * rows * width * width, bytes_accessed=2 * width * width + 10 * rows * width, transcendentals=0
        ),
        name="model_rows",
    )(place, held, *own, *other, momentum)


def swap(value, axis):
    return lax.ppermute(value, axis, [(0, 1), (1, 0)])


def across(value):
    return lax.ppermute(value, ("yh", "yl"), [(place, 3 - place) for place in range(4)])


def along_z(value, step):
    n = SIZES[0]
    return lax.ppermute(value, "z", [(i, (i + step) % n) for i in range(n)])


def exchange(value):
    return lax.all_to_all(value, EXP, split_axis=0, concat_axis=0, tiled=True)


def per_device(grad_block, momentum, model_root, expert_root):
    experts, hidden, width = grad_block.shape
    rows = experts * hidden
    half = width // 2
    z, yh, core = (lax.axis_index(axis) for axis in ("z", "yh", "core"))

    mine = lax.dynamic_slice_in_dim(model_root, core * half, half, axis=1).T
    sent = sliced(grad_block.reshape(rows, width), experts, hidden)
    mine, sent = lax.optimization_barrier((mine, sent))
    near, far = {0: mine}, {}

    def spread(shares, distance):
        shares[distance] = along_z(shares[distance - 1], -1)
        shares[-distance] = along_z(shares[1 - distance], 1)

    def cross(*places):
        for place in places:
            far[place] = across(near[place])

    held = exchange(sent)
    spread(near, 1)
    cross(0)
    spread(near, 2)
    cross(1, -1)
    others = {0: [swap(near[0], "core"), swap(far[0], "core")]}
    held, others, near[2], near[-2], far[1], far[-1] = lax.optimization_barrier(
        (held, others, near[2], near[-2], far[1], far[-1])
    )

    blended = mixed_experts(expert_root, held.reshape(PARTS, hidden, experts, LANES))
    blended, near[2], near[-2] = lax.optimization_barrier((blended, near[2], near[-2]))

    back = exchange(blended.reshape(PARTS, rows, LANES))
    spread(near, 3)
    cross(2, -2)
    early = [shares[place] for place in OFFSETS[1:5] for shares in (near, far)]
    near[4] = along_z(near[-3], 1)
    spread(far, 3)
    cross(4)
    early, near[3], near[-3] = lax.optimization_barrier((early, near[3], near[-3]))
    for index, place in enumerate(OFFSETS[1:5]):
        others[place] = [swap(piece, "core") for piece in early[2 * index : 2 * index + 2]]
    for place in OFFSETS[5:]:
        others[place] = [swap(shares[place], "core") for shares in (near, far)]
    own = [shares[place] for place in OFFSETS for shares in (near, far)]
    other = [piece for place in OFFSETS for piece in others[place]]

    order = [lax.rem(z + SIZES[0] + offset, SIZES[0]) for offset in OFFSETS]
    place = jnp.stack([yh, core, *order]).astype(jnp.int32)
    out = finished(place, back, own, other, momentum.reshape(rows, width), experts, hidden)
    return out.reshape(experts, hidden, width)


def solution(mesh):
    fine = Mesh(mesh.devices.reshape(SIZES), NAMES)
    placed = (P(EXP, BLK, None), P(EXP, BLK, None), P(BLK, None), P())
    return jax.shard_map(
        per_device, mesh=fine, in_specs=placed, out_specs=P(EXP, BLK, None), check_vma=False
    )
```

```python
import jax
import jax.numpy as jnp
from jax import lax
from jax.experimental import pallas as pl
from jax.experimental.pallas import tpu as pltpu
from jax.sharding import Mesh, PartitionSpec as P

NAMES = ("z", "yh", "x", "yl", "core")
SIZES = (8, 2, 4, 2, 2)
EXP = ("x", "yl", "core")
BLK = ("z", "yh")
PARTS = 16
GROUP = 4
LANES = 128
MIB = 1024 * 1024
OFFSETS = (0, 1, -1, 2, -2, 3, -3, 4)
VMEM = pl.BlockSpec(memory_space=pltpu.VMEM)
ANY = pl.BlockSpec(memory_space=pl.ANY)


def order_matrix(rows, outer, inner):
    row = lax.broadcasted_iota(jnp.int32, (rows, 1), 0)
    source = (row & (outer - 1)) * inner + lax.shift_right_logical(row, outer.bit_length() - 1)
    column = lax.broadcasted_iota(jnp.int32, (rows, rows), 1)
    return jnp.where(source == column, 1.0, 0.0).astype(jnp.bfloat16)


def slice_kernel(experts, hidden, grad_ref, out_ref, grad, parts, in_sems, out_sems):
    groups, rows, columns = grad.shape

    def arrival(group):
        lanes = pl.ds(group * columns, columns)
        return pltpu.make_async_copy(grad_ref.at[:, lanes], grad.at[group], in_sems.at[group])

    def departure(group):
        there = pl.ds(group * GROUP, GROUP)
        return pltpu.make_async_copy(parts.at[there], out_ref.at[there], out_sems.at[group])

    for group in range(groups):
        arrival(group).start()
    order = order_matrix(rows, experts, hidden)
    for group in range(groups):
        arrival(group).wait()
        moved = jnp.dot(order, grad[group], preferred_element_type=jnp.float32).astype(jnp.bfloat16)
        for k in range(GROUP):
            parts[group * GROUP + k] = moved[:, k * LANES : (k + 1) * LANES]
        departure(group).start()
    for group in range(groups):
        departure(group).wait()


def sliced(grad, experts, hidden):
    rows, width = grad.shape
    groups = PARTS // GROUP
    shape = (PARTS, rows, LANES)
    return pl.pallas_call(
        lambda *refs: slice_kernel(experts, hidden, *refs),
        out_shape=jax.ShapeDtypeStruct(shape, jnp.bfloat16),
        in_specs=[ANY],
        out_specs=ANY,
        scratch_shapes=[
            pltpu.VMEM((groups, rows, GROUP * LANES), jnp.bfloat16),
            pltpu.VMEM(shape, jnp.bfloat16),
            pltpu.SemaphoreType.DMA((groups,)),
            pltpu.SemaphoreType.DMA((groups,)),
        ],
        compiler_params=pltpu.CompilerParams(vmem_limit_bytes=58 * MIB),
        cost_estimate=pl.CostEstimate(
            flops=2 * rows * rows * width, bytes_accessed=4 * rows * width, transcendentals=0
        ),
        name="slice_columns",
    )(grad)


def mix_kernel(root_ref, in_ref, out_ref, root, mixed, in_sem, out_sems):
    groups, hidden, experts, lanes = in_ref.shape

    def departure(h):
        there = (slice(None), pl.ds(h, GROUP))
        return pltpu.make_async_copy(mixed.at[there], out_ref.at[there], out_sems.at[h // GROUP])

    arrival = pltpu.make_async_copy(root_ref, root, in_sem)
    arrival.start()
    arrival.wait()
    for h in range(0, hidden, GROUP):
        some = jnp.concatenate([in_ref[:, h + k].reshape(groups * experts, lanes) for k in range(GROUP)], axis=1)
        sums = jnp.dot(root[...], some, preferred_element_type=jnp.float32).astype(jnp.bfloat16)
        for k in range(GROUP):
            mixed[:, h + k] = sums[:, k * lanes : (k + 1) * lanes].reshape(groups, experts, lanes)
        departure(h).start()
    for h in range(0, hidden, GROUP):
        departure(h).wait()


def mixed_experts(expert_root, held):
    groups, hidden, experts, lanes = held.shape
    total = groups * experts
    return pl.pallas_call(
        mix_kernel,
        out_shape=jax.ShapeDtypeStruct(held.shape, jnp.bfloat16),
        in_specs=[ANY, VMEM],
        out_specs=ANY,
        scratch_shapes=[
            pltpu.VMEM((total, total), jnp.bfloat16),
            pltpu.VMEM(held.shape, jnp.bfloat16),
            pltpu.SemaphoreType.DMA,
            pltpu.SemaphoreType.DMA((hidden // GROUP,)),
        ],
        compiler_params=pltpu.CompilerParams(vmem_limit_bytes=24 * MIB),
        cost_estimate=pl.CostEstimate(flops=0, bytes_accessed=0, transcendentals=0),
        name="mix_experts",
    )(expert_root, held)


def finish_kernel(experts, hidden, pieces, place_ref, held_ref, *refs):
    sources = refs[:pieces], refs[pieces : 2 * pieces]
    momentum_ref, out_ref, held, rows_of, roots, momentum, out = refs[2 * pieces : 2 * pieces + 7]
    held_sem, root_sems, momentum_sems, out_sems = refs[2 * pieces + 7 :]
    steps, rows, columns = out.shape
    per_half = PARTS // 2
    yh, core = place_ref[0], place_ref[1]

    def block(ref, step):
        return ref.at[:, pl.ds(pl.multiple_of(place_ref[2 + step] * columns, columns), columns)]

    def root_arrivals(side, step):
        pieces_of, sem = sources[side], root_sems.at[side]
        return [
            pltpu.make_async_copy(pieces_of[2 * step + k], roots.at[side, step, k], sem.at[2 * step + k])
            for k in range(2)
        ]

    def momentum_arrival(step):
        return pltpu.make_async_copy(block(momentum_ref, step), momentum.at[step], momentum_sems.at[step])

    def departure(step):
        return pltpu.make_async_copy(out.at[step], block(out_ref, step), out_sems.at[step])

    held_arrival = pltpu.make_async_copy(held_ref, held, held_sem)
    held_arrival.start()
    for step in range(steps):
        for copy in (*root_arrivals(0, step), *root_arrivals(1, step), momentum_arrival(step)):
            copy.start()
    order = order_matrix(rows, hidden, experts)
    held_arrival.wait()
    for part in range(0, PARTS, GROUP):
        some = jnp.concatenate([held[part + k] for k in range(GROUP)], axis=1)
        moved = jnp.dot(order, some, preferred_element_type=jnp.float32).astype(jnp.bfloat16)
        at = (part % per_half) * LANES
        rows_of[part // per_half, :, at : at + GROUP * LANES] = moved
    def product(first):
        both = (first, first + 1)
        total = None
        for step in both:
            for copy in (*root_arrivals(0, step), *root_arrivals(1, step), momentum_arrival(step)):
                copy.wait()
        for side, which in ((0, core), (1, 1 - core)):
            root = jnp.concatenate([roots[side, step, k] for step in both for k in range(2)], axis=1)
            term = jnp.dot(rows_of[which], root, preferred_element_type=jnp.float32)
            total = term if total is None else total + term
        return total

    def put(first, total):
        for step in (first, first + 1):
            for k, block_at in ((0, yh), (1, 1 - yh)):
                lanes = pl.ds(pl.multiple_of(block_at * LANES, LANES), LANES)
                at = ((step - first) * 2 + k) * LANES
                out[step, :, lanes] = 0.9 * momentum[step, :, lanes] + total[:, at : at + LANES]
            departure(step).start()

    total = product(0)
    for first in range(2, steps, 2):
        later = product(first)
        put(first - 2, total)
        total = later
    put(steps - 2, total)
    for step in range(steps):
        departure(step).wait()


def finished(place, held, own, other, momentum, experts, hidden):
    parts, rows, lanes = held.shape
    width = parts * lanes
    columns = 2 * LANES
    pieces, steps = len(own), len(OFFSETS)
    return pl.pallas_call(
        lambda *refs: finish_kernel(experts, hidden, pieces, *refs),
        out_shape=jax.ShapeDtypeStruct(momentum.shape, jnp.float32),
        in_specs=[pl.BlockSpec(memory_space=pltpu.SMEM), ANY, *[ANY] * (2 * pieces), ANY],
        out_specs=ANY,
        scratch_shapes=[
            pltpu.VMEM(held.shape, jnp.bfloat16),
            pltpu.VMEM((2, rows, width // 2), jnp.bfloat16),
            pltpu.VMEM((2, steps, 2, *own[0].shape), jnp.bfloat16),
            pltpu.VMEM((steps, rows, columns), jnp.float32),
            pltpu.VMEM((steps, rows, columns), jnp.float32),
            pltpu.SemaphoreType.DMA,
            pltpu.SemaphoreType.DMA((2, pieces)),
            pltpu.SemaphoreType.DMA((steps,)),
            pltpu.SemaphoreType.DMA((steps,)),
        ],
        compiler_params=pltpu.CompilerParams(vmem_limit_bytes=52 * MIB),
        cost_estimate=pl.CostEstimate(
            flops=2 * rows * width * width, bytes_accessed=2 * width * width + 10 * rows * width, transcendentals=0
        ),
        name="model_rows",
    )(place, held, *own, *other, momentum)


def swap(value, axis):
    return lax.ppermute(value, axis, [(0, 1), (1, 0)])


def across(value):
    return lax.ppermute(value, ("yh", "yl"), [(place, 3 - place) for place in range(4)])


def along_z(value, step):
    n = SIZES[0]
    return lax.ppermute(value, "z", [(i, (i + step) % n) for i in range(n)])


def exchange(value):
    return lax.all_to_all(value, EXP, split_axis=0, concat_axis=0, tiled=True)


def per_device(grad_block, momentum, model_root, expert_root):
    experts, hidden, width = grad_block.shape
    rows = experts * hidden
    half = width // 2
    z, yh, core = (lax.axis_index(axis) for axis in ("z", "yh", "core"))

    mine = lax.dynamic_slice_in_dim(model_root, core * half, half, axis=1).T
    sent = sliced(grad_block.reshape(rows, width), experts, hidden)
    mine, sent = lax.optimization_barrier((mine, sent))
    near, far = {0: mine}, {}

    def spread(shares, distance):
        shares[distance] = along_z(shares[distance - 1], -1)
        shares[-distance] = along_z(shares[1 - distance], 1)

    def cross(*places):
        for place in places:
            far[place] = across(near[place])

    held = exchange(sent)
    spread(near, 1)
    cross(0)
    spread(near, 2)
    cross(1, -1)
    others = {0: [swap(near[0], "core"), swap(far[0], "core")]}
    held, others, near[2], near[-2], far[1], far[-1] = lax.optimization_barrier(
        (held, others, near[2], near[-2], far[1], far[-1])
    )

    blended = mixed_experts(expert_root, held.reshape(PARTS, hidden, experts, LANES))
    blended, near[2], near[-2] = lax.optimization_barrier((blended, near[2], near[-2]))

    back = exchange(blended.reshape(PARTS, rows, LANES))
    spread(near, 3)
    cross(2, -2)
    early = [shares[place] for place in OFFSETS[1:5] for shares in (near, far)]
    near[4] = along_z(near[-3], 1)
    spread(far, 3)
    cross(4)
    early, near[3], near[-3] = lax.optimization_barrier((early, near[3], near[-3]))
    for index, place in enumerate(OFFSETS[1:5]):
        others[place] = [swap(piece, "core") for piece in early[2 * index : 2 * index + 2]]
    for place in OFFSETS[5:]:
        others[place] = [swap(shares[place], "core") for shares in (near, far)]
    own = [shares[place] for place in OFFSETS for shares in (near, far)]
    other = [piece for place in OFFSETS for piece in others[place]]

    order = [lax.rem(z + SIZES[0] + offset, SIZES[0]) for offset in OFFSETS]
    place = jnp.stack([yh, core, *order]).astype(jnp.int32)
    out = finished(place, back, own, other, momentum.reshape(rows, width), experts, hidden)
    return out.reshape(experts, hidden, width)


def solution(mesh):
    fine = Mesh(mesh.devices.reshape(SIZES), NAMES)
    placed = (P(EXP, BLK, None), P(EXP, BLK, None), P(BLK, None), P())
    return jax.shard_map(
        per_device, mesh=fine, in_specs=placed, out_specs=P(EXP, BLK, None), check_vma=False
    )
```

```python
import jax
import jax.numpy as jnp
from jax import lax
from jax.experimental import pallas as pl
from jax.experimental.pallas import tpu as pltpu
from jax.sharding import Mesh, PartitionSpec as P

NAMES = ("z", "yh", "x", "yl", "core")
SIZES = (8, 2, 4, 2, 2)
EXP = ("x", "yl", "core")
BLK = ("z", "yh")
PARTS = 16
GROUP = 4
LANES = 128
MIB = 1024 * 1024
OFFSETS = (0, 1, -1, 2, -2, 3, -3, 4)
VMEM = pl.BlockSpec(memory_space=pltpu.VMEM)
ANY = pl.BlockSpec(memory_space=pl.ANY)


def order_matrix(rows, outer, inner):
    row = lax.broadcasted_iota(jnp.int32, (rows, 1), 0)
    source = (row & (outer - 1)) * inner + lax.shift_right_logical(row, outer.bit_length() - 1)
    column = lax.broadcasted_iota(jnp.int32, (rows, rows), 1)
    return jnp.where(source == column, 1.0, 0.0).astype(jnp.bfloat16)


def slice_kernel(experts, hidden, grad_ref, out_ref, grad, parts, in_sems, out_sems):
    groups, rows, columns = grad.shape

    def arrival(group):
        lanes = pl.ds(group * columns, columns)
        return pltpu.make_async_copy(grad_ref.at[:, lanes], grad.at[group], in_sems.at[group])

    def departure(group):
        there = pl.ds(group * GROUP, GROUP)
        return pltpu.make_async_copy(parts.at[there], out_ref.at[there], out_sems.at[group])

    for group in range(groups):
        arrival(group).start()
    order = order_matrix(rows, experts, hidden)
    for group in range(groups):
        arrival(group).wait()
        moved = jnp.dot(order, grad[group], preferred_element_type=jnp.float32).astype(jnp.bfloat16)
        for k in range(GROUP):
            parts[group * GROUP + k] = moved[:, k * LANES : (k + 1) * LANES]
        departure(group).start()
    for group in range(groups):
        departure(group).wait()


def sliced(grad, experts, hidden):
    rows, width = grad.shape
    groups = PARTS // GROUP
    shape = (PARTS, rows, LANES)
    return pl.pallas_call(
        lambda *refs: slice_kernel(experts, hidden, *refs),
        out_shape=jax.ShapeDtypeStruct(shape, jnp.bfloat16),
        in_specs=[ANY],
        out_specs=ANY,
        scratch_shapes=[
            pltpu.VMEM((groups, rows, GROUP * LANES), jnp.bfloat16),
            pltpu.VMEM(shape, jnp.bfloat16),
            pltpu.SemaphoreType.DMA((groups,)),
            pltpu.SemaphoreType.DMA((groups,)),
        ],
        compiler_params=pltpu.CompilerParams(vmem_limit_bytes=58 * MIB),
        cost_estimate=pl.CostEstimate(
            flops=2 * rows * rows * width, bytes_accessed=4 * rows * width, transcendentals=0
        ),
        name="slice_columns",
    )(grad)


def mix_kernel(root_ref, in_ref, out_ref, root, mixed, in_sem, out_sems):
    groups, hidden, experts, lanes = in_ref.shape

    def departure(h):
        there = (slice(None), pl.ds(h, GROUP))
        return pltpu.make_async_copy(mixed.at[there], out_ref.at[there], out_sems.at[h // GROUP])

    arrival = pltpu.make_async_copy(root_ref, root, in_sem)
    arrival.start()
    arrival.wait()
    for h in range(0, hidden, GROUP):
        some = jnp.concatenate([in_ref[:, h + k].reshape(groups * experts, lanes) for k in range(GROUP)], axis=1)
        sums = jnp.dot(root[...], some, preferred_element_type=jnp.float32).astype(jnp.bfloat16)
        for k in range(GROUP):
            mixed[:, h + k] = sums[:, k * lanes : (k + 1) * lanes].reshape(groups, experts, lanes)
        departure(h).start()
    for h in range(0, hidden, GROUP):
        departure(h).wait()


def mixed_experts(expert_root, held):
    groups, hidden, experts, lanes = held.shape
    total = groups * experts
    return pl.pallas_call(
        mix_kernel,
        out_shape=jax.ShapeDtypeStruct(held.shape, jnp.bfloat16),
        in_specs=[ANY, VMEM],
        out_specs=ANY,
        scratch_shapes=[
            pltpu.VMEM((total, total), jnp.bfloat16),
            pltpu.VMEM(held.shape, jnp.bfloat16),
            pltpu.SemaphoreType.DMA,
            pltpu.SemaphoreType.DMA((hidden // GROUP,)),
        ],
        compiler_params=pltpu.CompilerParams(vmem_limit_bytes=24 * MIB),
        cost_estimate=pl.CostEstimate(flops=0, bytes_accessed=0, transcendentals=0),
        name="mix_experts",
    )(expert_root, held)


def finish_kernel(experts, hidden, pieces, place_ref, held_ref, *refs):
    sources = refs[:pieces], refs[pieces : 2 * pieces]
    momentum_ref, out_ref, held, rows_of, roots, momentum, out = refs[2 * pieces : 2 * pieces + 7]
    held_sem, root_sems, momentum_sems, out_sems = refs[2 * pieces + 7 :]
    steps, rows, columns = out.shape
    per_half = PARTS // 2
    yh, core = place_ref[0], place_ref[1]

    def block(ref, step):
        return ref.at[:, pl.ds(pl.multiple_of(place_ref[2 + step] * columns, columns), columns)]

    def root_arrivals(side, step):
        pieces_of, sem = sources[side], root_sems.at[side]
        return [
            pltpu.make_async_copy(pieces_of[2 * step + k], roots.at[side, step, k], sem.at[2 * step + k])
            for k in range(2)
        ]

    def momentum_arrival(step):
        return pltpu.make_async_copy(block(momentum_ref, step), momentum.at[step], momentum_sems.at[step])

    def departure(step):
        return pltpu.make_async_copy(out.at[step], block(out_ref, step), out_sems.at[step])

    held_arrival = pltpu.make_async_copy(held_ref, held, held_sem)
    held_arrival.start()
    for step in range(steps):
        for copy in (*root_arrivals(0, step), *root_arrivals(1, step), momentum_arrival(step)):
            copy.start()
    order = order_matrix(rows, hidden, experts)
    held_arrival.wait()
    for part in range(0, PARTS, GROUP):
        some = jnp.concatenate([held[part + k] for k in range(GROUP)], axis=1)
        moved = jnp.dot(order, some, preferred_element_type=jnp.float32).astype(jnp.bfloat16)
        at = (part % per_half) * LANES
        rows_of[part // per_half, :, at : at + GROUP * LANES] = moved
    def product(first):
        both = (first, first + 1)
        total = None
        for step in both:
            for copy in (*root_arrivals(0, step), *root_arrivals(1, step), momentum_arrival(step)):
                copy.wait()
        for side, which in ((0, core), (1, 1 - core)):
            root = jnp.concatenate([roots[side, step, k] for step in both for k in range(2)], axis=1)
            term = jnp.dot(rows_of[which], root, preferred_element_type=jnp.float32)
            total = term if total is None else total + term
        return total

    def put(first, total):
        for step in (first, first + 1):
            for k, block_at in ((0, yh), (1, 1 - yh)):
                lanes = pl.ds(pl.multiple_of(block_at * LANES, LANES), LANES)
                at = ((step - first) * 2 + k) * LANES
                out[step, :, lanes] = 0.9 * momentum[step, :, lanes] + total[:, at : at + LANES]
            departure(step).start()

    total = product(0)
    for first in range(2, steps, 2):
        later = product(first)
        put(first - 2, total)
        total = later
    put(steps - 2, total)
    for step in range(steps):
        departure(step).wait()


def finished(place, held, own, other, momentum, experts, hidden):
    parts, rows, lanes = held.shape
    width = parts * lanes
    columns = 2 * LANES
    pieces, steps = len(own), len(OFFSETS)
    return pl.pallas_call(
        lambda *refs: finish_kernel(experts, hidden, pieces, *refs),
        out_shape=jax.ShapeDtypeStruct(momentum.shape, jnp.float32),
        in_specs=[pl.BlockSpec(memory_space=pltpu.SMEM), ANY, *[ANY] * (2 * pieces), ANY],
        out_specs=ANY,
        scratch_shapes=[
            pltpu.VMEM(held.shape, jnp.bfloat16),
            pltpu.VMEM((2, rows, width // 2), jnp.bfloat16),
            pltpu.VMEM((2, steps, 2, *own[0].shape), jnp.bfloat16),
            pltpu.VMEM((steps, rows, columns), jnp.float32),
            pltpu.VMEM((steps, rows, columns), jnp.float32),
            pltpu.SemaphoreType.DMA,
            pltpu.SemaphoreType.DMA((2, pieces)),
            pltpu.SemaphoreType.DMA((steps,)),
            pltpu.SemaphoreType.DMA((steps,)),
        ],
        compiler_params=pltpu.CompilerParams(vmem_limit_bytes=52 * MIB),
        cost_estimate=pl.CostEstimate(
            flops=2 * rows * width * width, bytes_accessed=2 * width * width + 10 * rows * width, transcendentals=0
        ),
        name="model_rows",
    )(place, held, *own, *other, momentum)


def swap(value, axis):
    return lax.ppermute(value, axis, [(0, 1), (1, 0)])


def across(value):
    return lax.ppermute(value, ("yh", "yl"), [(place, 3 - place) for place in range(4)])


def along_z(value, step):
    n = SIZES[0]
    return lax.ppermute(value, "z", [(i, (i + step) % n) for i in range(n)])


def exchange(value):
    return lax.all_to_all(value, EXP, split_axis=0, concat_axis=0, tiled=True)


def per_device(grad_block, momentum, model_root, expert_root):
    experts, hidden, width = grad_block.shape
    rows = experts * hidden
    half = width // 2
    z, yh, core = (lax.axis_index(axis) for axis in ("z", "yh", "core"))

    mine = lax.dynamic_slice_in_dim(model_root, core * half, half, axis=1).T
    sent = sliced(grad_block.reshape(rows, width), experts, hidden)
    mine, sent = lax.optimization_barrier((mine, sent))
    near, far = {0: mine}, {}

    def spread(shares, distance):
        shares[distance] = along_z(shares[distance - 1], -1)
        shares[-distance] = along_z(shares[1 - distance], 1)

    def cross(*places):
        for place in places:
            far[place] = across(near[place])

    held = exchange(sent)
    spread(near, 1)
    cross(0)
    spread(near, 2)
    cross(1, -1)
    others = {0: [swap(near[0], "core"), swap(far[0], "core")]}
    side = [swap(near[place], "core") for place in (1, -1)]
    held, others, side, near[2], near[-2], far[1], far[-1] = lax.optimization_barrier(
        (held, others, side, near[2], near[-2], far[1], far[-1])
    )

    blended = mixed_experts(expert_root, held.reshape(PARTS, hidden, experts, LANES))
    blended, near[2], near[-2] = lax.optimization_barrier((blended, near[2], near[-2]))

    back = exchange(blended.reshape(PARTS, rows, LANES))
    spread(near, 3)
    cross(2, -2)
    early = [shares[place] for place in OFFSETS[1:5] for shares in (near, far)]
    near[4] = along_z(near[-3], 1)
    spread(far, 3)
    far[4] = along_z(far[3], -1)
    early, near[3], near[-3] = lax.optimization_barrier((early, near[3], near[-3]))
    for index, place in enumerate(OFFSETS[1:5]):
        others[place] = [
            side[index] if index < 2 else swap(early[2 * index], "core"),
            swap(early[2 * index + 1], "core"),
        ]
    for place in OFFSETS[5:]:
        others[place] = [swap(shares[place], "core") for shares in (near, far)]
    own = [shares[place] for place in OFFSETS for shares in (near, far)]
    other = [piece for place in OFFSETS for piece in others[place]]

    order = [lax.rem(z + SIZES[0] + offset, SIZES[0]) for offset in OFFSETS]
    place = jnp.stack([yh, core, *order]).astype(jnp.int32)
    out = finished(place, back, own, other, momentum.reshape(rows, width), experts, hidden)
    return out.reshape(experts, hidden, width)


def solution(mesh):
    fine = Mesh(mesh.devices.reshape(SIZES), NAMES)
    placed = (P(EXP, BLK, None), P(EXP, BLK, None), P(BLK, None), P())
    return jax.shard_map(
        per_device, mesh=fine, in_specs=placed, out_specs=P(EXP, BLK, None), check_vma=False
    )
```

```python
import jax
import jax.numpy as jnp
from jax import lax
from jax.experimental import pallas as pl
from jax.experimental.pallas import tpu as pltpu
from jax.sharding import Mesh, PartitionSpec as P

NAMES = ("z", "yh", "x", "yl", "core")
SIZES = (8, 2, 4, 2, 2)
EXP = ("x", "yl", "core")
BLK = ("z", "yh")
PARTS = 16
GROUP = 4
LANES = 128
MIB = 1024 * 1024
OFFSETS = (0, 1, -1, 2, -2, 3, -3, 4)
VMEM = pl.BlockSpec(memory_space=pltpu.VMEM)
ANY = pl.BlockSpec(memory_space=pl.ANY)


def order_matrix(rows, outer, inner):
    row = lax.broadcasted_iota(jnp.int32, (rows, 1), 0)
    source = (row & (outer - 1)) * inner + lax.shift_right_logical(row, outer.bit_length() - 1)
    column = lax.broadcasted_iota(jnp.int32, (rows, rows), 1)
    return jnp.where(source == column, 1.0, 0.0).astype(jnp.bfloat16)


def slice_kernel(experts, hidden, grad_ref, out_ref, grad, parts, in_sems, out_sems):
    groups, rows, columns = grad.shape

    def arrival(group):
        lanes = pl.ds(group * columns, columns)
        return pltpu.make_async_copy(grad_ref.at[:, lanes], grad.at[group], in_sems.at[group])

    def departure(group):
        there = pl.ds(group * GROUP, GROUP)
        return pltpu.make_async_copy(parts.at[there], out_ref.at[there], out_sems.at[group])

    for group in range(groups):
        arrival(group).start()
    order = order_matrix(rows, experts, hidden)
    for group in range(groups):
        arrival(group).wait()
        moved = jnp.dot(order, grad[group], preferred_element_type=jnp.float32).astype(jnp.bfloat16)
        for k in range(GROUP):
            parts[group * GROUP + k] = moved[:, k * LANES : (k + 1) * LANES]
        departure(group).start()
    for group in range(groups):
        departure(group).wait()


def sliced(grad, experts, hidden):
    rows, width = grad.shape
    groups = PARTS // GROUP
    shape = (PARTS, rows, LANES)
    return pl.pallas_call(
        lambda *refs: slice_kernel(experts, hidden, *refs),
        out_shape=jax.ShapeDtypeStruct(shape, jnp.bfloat16),
        in_specs=[ANY],
        out_specs=ANY,
        scratch_shapes=[
            pltpu.VMEM((groups, rows, GROUP * LANES), jnp.bfloat16),
            pltpu.VMEM(shape, jnp.bfloat16),
            pltpu.SemaphoreType.DMA((groups,)),
            pltpu.SemaphoreType.DMA((groups,)),
        ],
        compiler_params=pltpu.CompilerParams(vmem_limit_bytes=58 * MIB),
        cost_estimate=pl.CostEstimate(
            flops=2 * rows * rows * width, bytes_accessed=4 * rows * width, transcendentals=0
        ),
        name="slice_columns",
    )(grad)


def mix_kernel(root_ref, in_ref, out_ref, root, mixed, in_sem, out_sems):
    groups, hidden, experts, lanes = in_ref.shape

    def departure(h):
        there = (slice(None), pl.ds(h, GROUP))
        return pltpu.make_async_copy(mixed.at[there], out_ref.at[there], out_sems.at[h // GROUP])

    arrival = pltpu.make_async_copy(root_ref, root, in_sem)
    arrival.start()
    arrival.wait()
    for h in range(0, hidden, GROUP):
        some = jnp.concatenate([in_ref[:, h + k].reshape(groups * experts, lanes) for k in range(GROUP)], axis=1)
        sums = jnp.dot(root[...], some, preferred_element_type=jnp.float32).astype(jnp.bfloat16)
        for k in range(GROUP):
            mixed[:, h + k] = sums[:, k * lanes : (k + 1) * lanes].reshape(groups, experts, lanes)
        departure(h).start()
    for h in range(0, hidden, GROUP):
        departure(h).wait()


def mixed_experts(expert_root, held):
    groups, hidden, experts, lanes = held.shape
    total = groups * experts
    return pl.pallas_call(
        mix_kernel,
        out_shape=jax.ShapeDtypeStruct(held.shape, jnp.bfloat16),
        in_specs=[ANY, VMEM],
        out_specs=ANY,
        scratch_shapes=[
            pltpu.VMEM((total, total), jnp.bfloat16),
            pltpu.VMEM(held.shape, jnp.bfloat16),
            pltpu.SemaphoreType.DMA,
            pltpu.SemaphoreType.DMA((hidden // GROUP,)),
        ],
        compiler_params=pltpu.CompilerParams(vmem_limit_bytes=24 * MIB),
        cost_estimate=pl.CostEstimate(flops=0, bytes_accessed=0, transcendentals=0),
        name="mix_experts",
    )(expert_root, held)


def finish_kernel(experts, hidden, pieces, place_ref, held_ref, *refs):
    sources = refs[:pieces], refs[pieces : 2 * pieces]
    momentum_ref, out_ref, held, rows_of, roots, momentum, out = refs[2 * pieces : 2 * pieces + 7]
    held_sem, root_sems, momentum_sems, out_sems = refs[2 * pieces + 7 :]
    steps, rows, columns = out.shape
    per_half = PARTS // 2
    yh, core = place_ref[0], place_ref[1]

    def block(ref, step):
        return ref.at[:, pl.ds(pl.multiple_of(place_ref[2 + step] * columns, columns), columns)]

    def root_arrivals(side, step):
        pieces_of, sem = sources[side], root_sems.at[side]
        return [
            pltpu.make_async_copy(pieces_of[2 * step + k], roots.at[side, step, k], sem.at[2 * step + k])
            for k in range(2)
        ]

    def momentum_arrival(step):
        return pltpu.make_async_copy(block(momentum_ref, step), momentum.at[step], momentum_sems.at[step])

    def departure(step):
        return pltpu.make_async_copy(out.at[step], block(out_ref, step), out_sems.at[step])

    def held_arrival(part):
        there = pl.ds(part, GROUP)
        return pltpu.make_async_copy(held_ref.at[there], held.at[there], held_sem.at[part // GROUP])

    for part in range(0, PARTS, GROUP):
        held_arrival(part).start()
    for step in range(steps):
        for copy in (*root_arrivals(0, step), *root_arrivals(1, step), momentum_arrival(step)):
            copy.start()
    order = order_matrix(rows, hidden, experts)
    for part in range(0, PARTS, GROUP):
        held_arrival(part).wait()
        some = jnp.concatenate([held[part + k] for k in range(GROUP)], axis=1)
        moved = jnp.dot(order, some, preferred_element_type=jnp.float32).astype(jnp.bfloat16)
        at = (part % per_half) * LANES
        rows_of[part // per_half, :, at : at + GROUP * LANES] = moved
    def product(first):
        both = (first, first + 1)
        total = None
        for step in both:
            for copy in (*root_arrivals(0, step), *root_arrivals(1, step), momentum_arrival(step)):
                copy.wait()
        for side, which in ((0, core), (1, 1 - core)):
            root = jnp.concatenate([roots[side, step, k] for step in both for k in range(2)], axis=1)
            term = jnp.dot(rows_of[which], root, preferred_element_type=jnp.float32)
            total = term if total is None else total + term
        return total

    def put(first, total):
        for step in (first, first + 1):
            for k, block_at in ((0, yh), (1, 1 - yh)):
                lanes = pl.ds(pl.multiple_of(block_at * LANES, LANES), LANES)
                at = ((step - first) * 2 + k) * LANES
                out[step, :, lanes] = 0.9 * momentum[step, :, lanes] + total[:, at : at + LANES]
            departure(step).start()

    total = product(0)
    for first in range(2, steps, 2):
        later = product(first)
        put(first - 2, total)
        total = later
    put(steps - 2, total)
    for step in range(steps):
        departure(step).wait()


def finished(place, held, own, other, momentum, experts, hidden):
    parts, rows, lanes = held.shape
    width = parts * lanes
    columns = 2 * LANES
    pieces, steps = len(own), len(OFFSETS)
    return pl.pallas_call(
        lambda *refs: finish_kernel(experts, hidden, pieces, *refs),
        out_shape=jax.ShapeDtypeStruct(momentum.shape, jnp.float32),
        in_specs=[pl.BlockSpec(memory_space=pltpu.SMEM), ANY, *[ANY] * (2 * pieces), ANY],
        out_specs=ANY,
        scratch_shapes=[
            pltpu.VMEM(held.shape, jnp.bfloat16),
            pltpu.VMEM((2, rows, width // 2), jnp.bfloat16),
            pltpu.VMEM((2, steps, 2, *own[0].shape), jnp.bfloat16),
            pltpu.VMEM((steps, rows, columns), jnp.float32),
            pltpu.VMEM((steps, rows, columns), jnp.float32),
            pltpu.SemaphoreType.DMA((PARTS // GROUP,)),
            pltpu.SemaphoreType.DMA((2, pieces)),
            pltpu.SemaphoreType.DMA((steps,)),
            pltpu.SemaphoreType.DMA((steps,)),
        ],
        compiler_params=pltpu.CompilerParams(vmem_limit_bytes=52 * MIB),
        cost_estimate=pl.CostEstimate(
            flops=2 * rows * width * width, bytes_accessed=2 * width * width + 10 * rows * width, transcendentals=0
        ),
        name="model_rows",
    )(place, held, *own, *other, momentum)


def swap(value, axis):
    return lax.ppermute(value, axis, [(0, 1), (1, 0)])


def across(value):
    return lax.ppermute(value, ("yh", "yl"), [(place, 3 - place) for place in range(4)])


def along_z(value, step):
    n = SIZES[0]
    return lax.ppermute(value, "z", [(i, (i + step) % n) for i in range(n)])


def exchange(value):
    return lax.all_to_all(value, EXP, split_axis=0, concat_axis=0, tiled=True)


def per_device(grad_block, momentum, model_root, expert_root):
    experts, hidden, width = grad_block.shape
    rows = experts * hidden
    half = width // 2
    z, yh, core = (lax.axis_index(axis) for axis in ("z", "yh", "core"))

    mine = lax.dynamic_slice_in_dim(model_root, core * half, half, axis=1).T
    sent = sliced(grad_block.reshape(rows, width), experts, hidden)
    mine, sent = lax.optimization_barrier((mine, sent))
    near, far = {0: mine}, {}

    def spread(shares, distance):
        shares[distance] = along_z(shares[distance - 1], -1)
        shares[-distance] = along_z(shares[1 - distance], 1)

    def cross(*places):
        for place in places:
            far[place] = across(near[place])

    held = exchange(sent)
    spread(near, 1)
    cross(0)
    spread(near, 2)
    cross(1, -1)
    others = {0: [swap(near[0], "core"), swap(far[0], "core")]}
    side = [swap(near[place], "core") for place in (1, -1)]
    held, others, side, near[2], near[-2], far[1], far[-1] = lax.optimization_barrier(
        (held, others, side, near[2], near[-2], far[1], far[-1])
    )

    blended = mixed_experts(expert_root, held.reshape(PARTS, hidden, experts, LANES))
    blended, near[2], near[-2] = lax.optimization_barrier((blended, near[2], near[-2]))

    back = exchange(blended.reshape(PARTS, rows, LANES))
    spread(near, 3)
    cross(2, -2)
    early = [shares[place] for place in OFFSETS[1:5] for shares in (near, far)]
    near[4] = along_z(near[-3], 1)
    spread(far, 3)
    far[4] = along_z(far[3], -1)
    early, near[3], near[-3] = lax.optimization_barrier((early, near[3], near[-3]))
    for index, place in enumerate(OFFSETS[1:5]):
        others[place] = [
            side[index] if index < 2 else swap(early[2 * index], "core"),
            swap(early[2 * index + 1], "core"),
        ]
    for place in OFFSETS[5:]:
        others[place] = [swap(shares[place], "core") for shares in (near, far)]
    own = [shares[place] for place in OFFSETS for shares in (near, far)]
    other = [piece for place in OFFSETS for piece in others[place]]

    order = [lax.rem(z + SIZES[0] + offset, SIZES[0]) for offset in OFFSETS]
    place = jnp.stack([yh, core, *order]).astype(jnp.int32)
    out = finished(place, back, own, other, momentum.reshape(rows, width), experts, hidden)
    return out.reshape(experts, hidden, width)


def solution(mesh):
    fine = Mesh(mesh.devices.reshape(SIZES), NAMES)
    placed = (P(EXP, BLK, None), P(EXP, BLK, None), P(BLK, None), P())
    return jax.shard_map(
        per_device, mesh=fine, in_specs=placed, out_specs=P(EXP, BLK, None), check_vma=False
    )
```
